512 devices in a mesh: row: 8 (over z_lo, core), col: 8 (over z_hi, x), freq: 8 (over y).
Axes of the slice: x: 4, y: 8, z: 8 (z_hi: 2, z_lo: 4; z = z_hi * 4 + z_lo), core: 2. Of those that a mesh axis runs over, the one named last changes fastest.
Arguments:
- voltages: bfloat16 [16, 4096, 1024], P('freq', ('row', 'col')), may hold values from -6 to 6
- pair_owner: int32 [136], replicated, may hold values from 0 to 3
- chan_level: int32 [16], P('freq'), may hold values from 0 to 7
- stencil_table: float32 [4, 8, 3], replicated, may hold values from 0.2 to 1
Outputs:
- smoothed: float32 [16, 2, 8, 64, 8, 4096], P('freq', None, None, ('row', 'col'))
The draws below stay inside these ranges and needn't reach their ends.
All inputs are finite; a program needn't handle non-finite values.
Results may differ from the reference program's by a relative error of at most 0.0003.
Values may be sent and summed in bfloat16 or wider, within the bound.
A program may use at most 64 MiB of HBM per device.

```python
import jax
import jax.numpy as jnp
from jax import lax

TIME = 512
SUBARRAYS = 4
LEVELS = 8
INPUTS = 4096
CHANNELS = 16
ROW_BLOCKS = 8
GROUP = 64
HALF = 256
STRIPE = 8
TILES = 16
PAIRS = 136


def with_ends(entries, rng, low, top_value):
    longest = entries.shape.index(max(entries.shape))
    spots = []
    for shift in (0, 1):
        where = [jax.random.randint(jax.random.fold_in(rng, axis), (), 0, length) for axis, length in enumerate(entries.shape)]
        where[longest] = (where[longest] + shift) % entries.shape[longest]
        spots.append(tuple(where))
    return entries.at[spots[0]].set(low).at[spots[1]].set(top_value)


def shard_levels(stream_key, extent, cuts, least, top_value):
    factor_of, own = 1.0, jax.random.fold_in(stream_key, 6)
    for dim, parts in cuts:
        draws = jnp.exp(jax.random.uniform(jax.random.fold_in(own, dim), (parts,), jnp.float32, least / len(cuts), top_value / len(cuts)))
        factor_of = factor_of * jnp.repeat(draws, extent[dim] // parts).reshape([-1 if axis == dim else 1 for axis in range(len(extent))])
    return factor_of


def noise(key, dims, scale, bound, shards=(), kind=jnp.bfloat16):
    result = jax.random.normal(key, dims, jnp.float32) * scale
    if len(shards) > 0:
        result = shard_levels(key, dims, shards, -0.22, 0.18) * result
    return jnp.clip(result, min=-bound, max=bound).astype(kind)


def setup_inputs(seed: int = 0) -> dict:
    seeds = jax.random.split(jax.random.key(seed), 5)
    voltages = noise(seeds[0], (CHANNELS, INPUTS, 2 * TIME), 1.0, 6.0, ((0, 8), (1, 64)))
    pair_owner = with_ends(jax.random.randint(seeds[1], (PAIRS,), 0, SUBARRAYS), jax.random.fold_in(seeds[1], 1), 0, SUBARRAYS - 1).astype(jnp.int32)
    chan_level = with_ends(jax.random.randint(seeds[2], (CHANNELS,), 0, LEVELS), jax.random.fold_in(seeds[2], 1), 0, LEVELS - 1).astype(jnp.int32)
    stencil_table = jnp.clip(jax.random.uniform(seeds[3], (SUBARRAYS, LEVELS, 3), jnp.float32, 0.2, 1.0), 0.2, 1.0)
    return dict(voltages=voltages, pair_owner=pair_owner, chan_level=chan_level, stencil_table=stencil_table)


def owner_grid(pair_owner):
    across = jnp.arange(TILES, dtype=jnp.int32)[:, None]
    downto = jnp.arange(TILES, dtype=jnp.int32)[None, :]
    lower_tile = jnp.minimum(across, downto)
    upper_tile = jnp.maximum(across, downto)
    position = lower_tile * TILES - (lower_tile * (lower_tile - 1)) // 2 + upper_tile - lower_tile
    return pair_owner[position.astype(jnp.int32)]


def reference(voltages, pair_owner, chan_level, stencil_table):
    def one_channel(samples_in):
        values = samples_in.astype(jnp.float32)
        turned = jnp.concatenate([values[:, TIME:], -values[:, :TIME]], axis=1)
        real_part = jnp.dot(values, values.T, precision=lax.Precision.HIGHEST)
        imag_part = jnp.dot(turned, values.T, precision=lax.Precision.HIGHEST)
        return jnp.stack([real_part, imag_part]) / TIME

    visibility = lax.map(one_channel, voltages)
    owners = owner_grid(pair_owner)

    def smooth_one(channel):
        lower_index = jnp.maximum(channel - 1, 0).astype(jnp.int32)
        upper_index = jnp.minimum(channel + 1, CHANNELS - 1).astype(jnp.int32)
        previous = jnp.where(channel > 0, visibility[lower_index], 0.0)
        following = jnp.where(channel < CHANNELS - 1, visibility[upper_index], 0.0)
        coeffs = jnp.transpose(stencil_table[owners, chan_level[channel]], (2, 0, 1))
        expanded = jnp.repeat(jnp.repeat(coeffs, HALF, axis=1), HALF, axis=2)
        current = visibility[channel]
        return expanded[0][None] * previous + expanded[1][None] * current + expanded[2][None] * following

    filtered = lax.map(smooth_one, jnp.arange(CHANNELS, dtype=jnp.int32))
    return filtered.reshape(CHANNELS, 2, ROW_BLOCKS, GROUP, STRIPE, INPUTS)
```

```python
import jax
import jax.numpy as jnp
from jax import lax
from jax.experimental import pallas as pl
from jax.experimental.pallas import tpu as pltpu
from jax.sharding import PartitionSpec as P

MESH = pl.DeviceIdType.MESH
FULL = 32760.0
FINE = 128.0
PAD = 16
SHARD = 64
UNIT = 2 * SHARD


def correlator_kernel(
    v_ref, owner_ref, level_ref, table_ref, out_ref,
    vb, stripes, rows_own, rows_mate, a2, gram, smooth, hsend, hrecv, psend, precv,
    rows_s, rows_r, mate_s, mate_r, z_s, z_r, x_s, x_r, d_s, d_r, h_s, h_r, p_s, p_r,
):
    row, col, freq = lax.axis_index("row"), lax.axis_index("col"), lax.axis_index("freq")
    freq_count = lax.axis_size("freq")
    core, z_lo = row % 2, row // 2
    x, z_hi = col % 4, col // 4
    z = z_hi * 4 + z_lo
    side = x // 2

    def at_z(there):
        return ((there % 4) * 2 + core, (there // 4) * 4 + x, freq)

    z_next, z_prev = at_z((z + 1) % 8), at_z((z + 7) % 8)
    x_mate = (row, z_hi * 4 + (x + 1 - 2 * (x % 2)), freq)
    p_mate = (row, z_hi * 4 + (x + 3 + 2 * (x % 2)) % 4, freq)
    sibling = (row + 1 - 2 * core, col, freq)
    f_next = (row, col, (freq + 1) % freq_count)
    f_prev = (row, col, (freq + freq_count - 1) % freq_count)
    diagonal = row == col

    own_half = pl.multiple_of((x % 2) * SHARD, SHARD)
    mate_half = pl.multiple_of((1 - x % 2) * SHARD, SHARD)

    def remote(src, dst, send, recv, device):
        return pltpu.make_async_remote_copy(
            src_ref=src, dst_ref=dst, send_sem=send, recv_sem=recv,
            device_id=device, device_id_type=MESH,
        )

    def row_copy(c):
        return remote(stripes.at[c], rows_own.at[row], rows_s.at[c], rows_r.at[row], (col, c, freq))

    def row_arrival(b):
        return remote(stripes.at[0], rows_own.at[b], rows_s.at[0], rows_r.at[b], (b, row, freq))

    def mate_copy():
        return remote(rows_own, rows_mate, mate_s.at[0], mate_r.at[0], p_mate)

    def z_copy(way, stream, t):
        before = (t - 1) if way == 0 else (9 - t) % 8
        after = t if way == 0 else 8 - t
        ch = 1 if stream == 2 else 0
        start, size = (mate_half if stream == 1 else own_half), SHARD
        first = 0
        if stream == 2 and t == 4:
            first, size = way * (SHARD // 2), SHARD // 2
        if t == 1 and stream != 1:
            src = v_ref.at[ch]
        else:
            src = vb.at[before, ch, pl.ds(start + first, size)]
        dst = vb.at[after, ch, pl.ds(start + first, size)]
        return remote(
            src, dst, z_s.at[way, stream, t - 1], z_r.at[way, stream, t - 1],
            z_next if way == 0 else z_prev,
        )

    def x_copy(d, ch):
        slot = 8 if ch == 0 else d
        src = v_ref.at[ch] if d == 0 else vb.at[d, ch, pl.ds(own_half, SHARD)]
        return remote(src, vb.at[d, ch, pl.ds(own_half, SHARD)], x_s.at[slot], x_r.at[slot], x_mate)

    def x_arrival(d, ch):
        slot = 8 if ch == 0 else d
        here = vb.at[d, ch, pl.ds(mate_half, SHARD)]
        return remote(here, here, x_s.at[slot], x_r.at[slot], x_mate)

    def d_copy(d, ch):
        return remote(
            vb.at[d, ch, pl.ds(0, UNIT)], vb.at[d, ch, pl.ds(UNIT, UNIT)],
            d_s.at[d, ch], d_r.at[d, ch], sibling,
        )

    def h_copy(d, ch):
        return remote(
            hsend.at[d, ch], hrecv.at[d, ch], h_s.at[d, ch], h_r.at[d, ch],
            f_prev if ch == 0 else f_next,
        )

    def p_copy(d):
        return remote(psend.at[d], precv.at[d], p_s.at[d], p_r.at[d], p_mate)

    def encode(source, target, top):
        step = jnp.ceil(FINE * jnp.log(jnp.maximum(top, 1e-36)))
        inverse = jnp.exp(step * (-1.0 / FINE))
        for r in range(0, 256, 32):
            value = source[pl.ds(r, 32), :]
            share = jnp.minimum(jnp.abs(value) * inverse, 1.0)
            root = share * lax.rsqrt(share + 1e-30) * FULL
            code = jnp.where(value < 0, -root, root)
            target[pl.ds(r, 32), :] = jnp.round(code).astype(jnp.int32).astype(jnp.int16)
        target[pl.ds(256, PAD), :] = jnp.broadcast_to(step, (PAD, 256)).astype(jnp.int32).astype(jnp.int16)

    def scale_of(message, lanes):
        step = message[pl.ds(256, PAD), lanes].astype(jnp.int32).astype(jnp.float32)
        return jnp.exp(step * (1.0 / FINE)) * (1.0 / (FULL * FULL))

    def decoded(message, r, lanes):
        code = message[pl.ds(r, 16), lanes].astype(jnp.int32).astype(jnp.float32)
        return code * jnp.abs(code)

    def fill_rows(source, dev):
        wide = source[...].astype(jnp.float32)
        for ch in range(2):
            part = wide[:, 8 * ch : 8 * ch + 8, :].reshape(64, 1024).astype(jnp.bfloat16)
            base = dev * 128
            a2[ch, base : base + 64, :] = part
            a2[ch, base + 64 : base + 128, :512] = part[:, 512:]
            a2[ch, base + 64 : base + 128, 512:] = -part[:, :512]

    def products(d):
        for ch in range(2):
            d_copy(d, ch).wait_recv()
        for ch in range(2):
            g = lax.dot_general(
                a2[ch], vb[d, ch], (((1,), (1,)), ((), ())), preferred_element_type=jnp.float32
            )
            gram[d, ch] = g
            encode(gram.at[d, ch], hsend.at[d, ch], jnp.max(jnp.abs(g), keepdims=True))
            h_copy(d, ch).start()

    def place(d, cr):
        there = (z - d + 8) % 8
        block = (there % 4) * 2 + (core if cr == 0 else 1 - core)
        return block, there // 4

    def smoothing(d):
        for ch in range(2):
            h_copy(d, ch).wait_recv()
        top = jnp.zeros((16, 128), jnp.float32)
        for cr in range(2):
            lanes = pl.ds(cr * UNIT, UNIT)
            block, high = place(d, cr)
            first = pl.multiple_of(block * 512 + high * 256 + side * UNIT, UNIT)
            tile = block * 2 + high
            scale_next = scale_of(hrecv.at[d, 0], lanes)
            scale_prev = scale_of(hrecv.at[d, 1], lanes)
            for pair in range(4):
                taps = []
                for b in (2 * pair, 2 * pair + 1):
                    mine = 2 * b + row // 4
                    low = jnp.minimum(mine, tile)
                    spot = low * 16 - low * (low - 1) // 2 + jnp.abs(mine - tile)
                    owner = owner_ref[spot]
                    taps.append(
                        [[table_ref[owner, level_ref[ch], k] * (1.0 / 512) for k in range(3)] for ch in range(2)]
                    )
                wide = [
                    [
                        jnp.concatenate(
                            [jnp.full((8, 128), taps[0][ch][k]), jnp.full((8, 128), taps[1][ch][k])], axis=0
                        )
                        for k in range(3)
                    ]
                    for ch in range(2)
                ]
                wide_prev = jnp.where(freq > 0, wide[0][0] * scale_prev, 0.0)
                wide_next = jnp.where(freq < freq_count - 1, wide[1][2] * scale_next, 0.0)
                for dev in range(2):
                    for part in range(2):
                        r = (dev * 2 + part) * 64 + pair * 16
                        g0 = gram[d, 0, pl.ds(r, 16), lanes]
                        g1 = gram[d, 1, pl.ds(r, 16), lanes]
                        before = decoded(hrecv.at[d, 1], r, lanes)
                        after = decoded(hrecv.at[d, 0], r, lanes)
                        f0 = wide_prev * before + wide[0][1] * g0 + wide[0][2] * g1
                        f1 = wide[1][0] * g0 + wide[1][1] * g1 + wide_next * after
                        if dev == 0:
                            for ch, value in ((0, f0), (1, f1)):
                                out_ref[ch, part, 2 * pair : 2 * pair + 2, 0, :, pl.ds(first, UNIT)] = (
                                    value.reshape(2, 8, 128)
                                )
                        else:
                            for ch, value in ((0, f0), (1, f1)):
                                smooth[pl.ds((ch * 2 + part) * 64 + pair * 16, 16), lanes] = value
                            top = jnp.maximum(top, jnp.maximum(jnp.abs(f0), jnp.abs(f1)))
        encode(smooth, psend.at[d], jnp.max(top, keepdims=True))
        p_copy(d).start()

    def delivery(d):
        p_copy(d).wait_recv()
        for cr in range(2):
            lanes = pl.ds(cr * UNIT, UNIT)
            block, high = place(d, cr)
            first = pl.multiple_of(block * 512 + high * 256 + (1 - side) * UNIT, UNIT)
            scale = scale_of(precv.at[d], lanes)
            for ch in range(2):
                for part in range(2):
                    for pair in range(4):
                        value = decoded(precv.at[d], (ch * 2 + part) * 64 + pair * 16, lanes) * scale
                        out_ref[ch, part, 2 * pair : 2 * pair + 2, 0, :, pl.ds(first, UNIT)] = (
                            value.reshape(2, 8, 128)
                        )

    barrier = pltpu.get_barrier_semaphore()
    for device in (z_next, z_prev, x_mate, p_mate, sibling, f_next, f_prev):
        pl.semaphore_signal(barrier, inc=1, device_id=device, device_id_type=MESH)
    for other in range(8):
        for device in ((col, other, freq), (other, row, freq)):
            @pl.when(jnp.logical_not(jnp.logical_and(device[0] == row, device[1] == col)))
            def _():
                pl.semaphore_signal(barrier, inc=1, device_id=device, device_id_type=MESH)

    narrow = v_ref[...]
    wide_v = narrow.astype(jnp.float32)
    for c in range(8):
        pieces = [wide_v[ch, 8 * c : 8 * c + 8, :] for ch in range(2)]
        stripes[c] = jnp.concatenate(pieces, axis=0).astype(jnp.bfloat16)
    for ch in range(2):
        vb[0, ch, pl.ds(own_half, SHARD), :] = narrow[ch]

    pl.semaphore_wait(barrier, 23 - 2 * jnp.where(diagonal, 1, 0))

    for c in range(8):
        @pl.when(jnp.logical_not(jnp.logical_and(diagonal, c == col)))
        def _():
            row_copy(c).start()

    @pl.when(diagonal)
    def _():
        rows_own[row] = stripes[col]

    x_copy(0, 0).start()
    for way in range(2):
        z_copy(way, 0, 1).start()
    x_copy(0, 1).start()
    for way in range(2):
        z_copy(way, 2, 1).start()

    x_arrival(0, 0).wait_recv()
    for way in range(2):
        z_copy(way, 1, 1).start()
    d_copy(0, 0).start()
    x_arrival(0, 1).wait_recv()
    d_copy(0, 1).start()

    for b in range(8):
        @pl.when(jnp.logical_not(jnp.logical_and(diagonal, b == row)))
        def _():
            row_arrival(b).wait_recv()
    mate_copy().start()
    fill_rows(rows_own, 0)
    mate_copy().wait_recv()
    fill_rows(rows_mate, 1)

    ready, smoothed = [0], []
    for t in range(1, 5):
        here = [t, 8 - t] if t < 4 else [4]
        for stream in range(3):
            ways = [0, 1]
            if t == 4 and stream < 2:
                ways = [stream]
            for way in ways:
                z_copy(way, stream, t).wait_recv()
                if t < 3 or (t == 3 and (stream == 2 or way == stream)):
                    z_copy(way, stream, t + 1).start()
            if stream == 0:
                for d in ready:
                    products(d)
            elif stream == 1:
                for d in here:
                    d_copy(d, 0).start()
                for d in smoothed:
                    delivery(d)
            else:
                for d in here:
                    x_copy(d, 1).start()
                for d in ready:
                    smoothing(d)
                for d in here:
                    x_arrival(d, 1).wait_recv()
                    d_copy(d, 1).start()
        smoothed, ready = ready, here
    products(4)
    for d in smoothed:
        delivery(d)
    smoothing(4)
    delivery(4)

    for c in range(8):
        @pl.when(jnp.logical_not(jnp.logical_and(diagonal, c == col)))
        def _():
            row_copy(c).wait_send()
    mate_copy().wait_send()
    x_copy(0, 0).wait_send()
    for t in range(1, 5):
        for way in range(2):
            for stream in range(3):
                if t < 4 or stream == 2 or way == stream:
                    z_copy(way, stream, t).wait_send()
    for d in range(8):
        x_copy(d, 1).wait_send()
        p_copy(d).wait_send()
        for ch in range(2):
            d_copy(d, ch).wait_send()
            h_copy(d, ch).wait_send()


def on_device(voltages, pair_owner, chan_level, stencil_table):
    vmem = pl.BlockSpec(memory_space=pltpu.VMEM)
    smem = pl.BlockSpec(memory_space=pltpu.SMEM)
    dma = pltpu.SemaphoreType.DMA
    return pl.pallas_call(
        correlator_kernel,
        out_shape=jax.ShapeDtypeStruct((2, 2, 8, 1, 8, 4096), jnp.float32),
        in_specs=[vmem, smem, smem, smem],
        out_specs=vmem,
        scratch_shapes=[
            pltpu.VMEM((8, 2, 256, 1024), jnp.bfloat16),
            pltpu.VMEM((8, 16, 1024), jnp.bfloat16),
            pltpu.VMEM((8, 16, 1024), jnp.bfloat16),
            pltpu.VMEM((8, 16, 1024), jnp.bfloat16),
            pltpu.VMEM((2, 256, 1024), jnp.bfloat16),
            pltpu.VMEM((8, 2, 256, 256), jnp.float32),
            pltpu.VMEM((256, 256), jnp.float32),
            pltpu.VMEM((8, 2, 256 + PAD, 256), jnp.int16),
            pltpu.VMEM((8, 2, 256 + PAD, 256), jnp.int16),
            pltpu.VMEM((8, 256 + PAD, 256), jnp.int16),
            pltpu.VMEM((8, 256 + PAD, 256), jnp.int16),
            dma((8,)), dma((8,)), dma((1,)), dma((1,)),
            dma((2, 3, 4)), dma((2, 3, 4)),
            dma((9,)), dma((9,)),
            dma((8, 2)), dma((8, 2)),
            dma((8, 2)), dma((8, 2)),
            dma((8,)), dma((8,)),
        ],
        compiler_params=pltpu.CompilerParams(
            collective_id=0, has_side_effects=True, vmem_limit_bytes=44 * 1024 * 1024
        ),
    )(voltages, pair_owner, chan_level, stencil_table)


def solution(mesh):
    in_specs = (P("freq", ("row", "col"), None), P(), P("freq"), P())
    out_specs = P("freq", None, None, ("row", "col"), None, None)
    return jax.shard_map(
        on_device, mesh=mesh, in_specs=in_specs, out_specs=out_specs, check_vma=False
    )
```

```python
import jax
import jax.numpy as jnp
from jax import lax
from jax.experimental import pallas as pl
from jax.experimental.pallas import tpu as pltpu
from jax.sharding import PartitionSpec as P

MESH = pl.DeviceIdType.MESH
FULL = 32760.0
FINE = 128.0
PAD = 16
SHARD = 64
UNIT = 2 * SHARD
FIRST = "rxcav"
ORDER = (
    "I0 R0 C1 I1", "A1 B1 M0 g0", "X1 g1 C2 Y1", "A2 g7 f0 X2", "B2 f1 g2 C3", "Y2 g6 A3 f7", "X3 B3 f2 C4",
    "g3 Y3 f6 A4", "g5 B4 X4 o0", "o1 g4 f3 o7", "f5 o2 o6 f4", "o3 o5 o4",
)


def correlator_kernel(
    v_hbm, owner_hbm, level_hbm, table_hbm, out_ref,
    owner_ref, level_ref, table_ref, vb, stripes, rows_own, rows_mate, a2, gram, smooth, hsend, hrecv, psend, precv,
    in_s, rows_s, rows_r, mate_s, mate_r, z_s, z_r, x_s, x_r, d_s, d_r, h_s, h_r, p_s, p_r,
):
    row, col, freq = lax.axis_index("row"), lax.axis_index("col"), lax.axis_index("freq")
    freq_count = lax.axis_size("freq")
    core, z_lo = row % 2, row // 2
    x, z_hi = col % 4, col // 4
    z = z_hi * 4 + z_lo
    side = x // 2

    def at_z(there):
        return ((there % 4) * 2 + core, (there // 4) * 4 + x, freq)

    z_next, z_prev = at_z((z + 1) % 8), at_z((z + 7) % 8)
    x_mate = (row, z_hi * 4 + (x + 1 - 2 * (x % 2)), freq)
    p_mate = (row, z_hi * 4 + (x + 3 + 2 * (x % 2)) % 4, freq)
    sibling = (row + 1 - 2 * core, col, freq)
    f_next = (row, col, (freq + 1) % freq_count)
    f_prev = (row, col, (freq + freq_count - 1) % freq_count)
    diagonal = row == col

    own_half = pl.multiple_of((x % 2) * SHARD, SHARD)
    mate_half = pl.multiple_of((1 - x % 2) * SHARD, SHARD)

    def remote(src, dst, send, recv, device):
        return pltpu.make_async_remote_copy(
            src_ref=src, dst_ref=dst, send_sem=send, recv_sem=recv,
            device_id=device, device_id_type=MESH,
        )

    def row_copy(c):
        return remote(stripes.at[c], rows_own.at[row], rows_s.at[0], rows_r.at[row], (col, c, freq))

    def row_arrival(b):
        return remote(stripes.at[0], rows_own.at[b], rows_s.at[0], rows_r.at[b], (b, row, freq))

    def mate_copy(b):
        return remote(rows_own.at[b], rows_mate.at[b], mate_s.at[0], mate_r.at[0], p_mate)

    def z_copy(way, stream, t):
        before = (t - 1) if way == 0 else (9 - t) % 8
        after = t if way == 0 else 8 - t
        ch = 1 if stream == 2 else 0
        start, size = (mate_half if stream == 1 else own_half), SHARD
        first = 0
        if stream == 2 and t == 4:
            first, size = way * (SHARD // 2), SHARD // 2
        src = vb.at[before, ch, pl.ds(start + first, size)]
        dst = vb.at[after, ch, pl.ds(start + first, size)]
        return remote(
            src, dst, z_s.at[0], z_r.at[way, stream, t - 1],
            z_next if way == 0 else z_prev,
        )

    def x_copy(d, ch):
        slot = 8 if ch == 0 else d
        part = vb.at[d, ch, pl.ds(own_half, SHARD)]
        return remote(part, part, x_s.at[0], x_r.at[slot], x_mate)

    def x_arrival(d, ch):
        slot = 8 if ch == 0 else d
        here = vb.at[d, ch, pl.ds(mate_half, SHARD)]
        return remote(here, here, x_s.at[0], x_r.at[slot], x_mate)

    def d_copy(d, ch, start):
        return remote(
            vb.at[d, ch, pl.ds(start, SHARD)], vb.at[d, ch, pl.ds(UNIT + start, SHARD)],
            d_s.at[0], d_r.at[d], sibling,
        )

    def d_arrival(d):
        here = vb.at[d, :, pl.ds(UNIT, UNIT)]
        return remote(here, here, d_s.at[0], d_r.at[d], sibling)

    def h_copy(d, ch, cr):
        return remote(
            hsend.at[d, cr, ch], hrecv.at[d, cr, ch], h_s.at[0], h_r.at[d, cr],
            f_prev if ch == 0 else f_next,
        )

    def h_arrival(d, cr):
        return remote(hsend.at[d, cr], hrecv.at[d, cr], h_s.at[0], h_r.at[d, cr], f_next)

    def p_copy(d, cr):
        return remote(psend.at[d, cr], precv.at[d, cr], p_s.at[0], p_r.at[d], p_mate)

    def p_arrival(d):
        return remote(psend.at[d], precv.at[d], p_s.at[0], p_r.at[d], p_mate)

    def all_left():
        @pl.when(diagonal)
        def _():
            some = stripes.at[pl.ds(0, 7)]
            remote(some, some, rows_s.at[0], rows_r.at[0], sibling).wait_send()

        @pl.when(jnp.logical_not(diagonal))
        def _():
            remote(stripes, stripes, rows_s.at[0], rows_r.at[0], sibling).wait_send()

        for sent, semaphore in (
            (rows_own, mate_s),
            (vb.at[pl.ds(0, 7), 0, pl.ds(0, 3 * SHARD)], z_s),
            (vb.at[pl.ds(0, 3), 0, pl.ds(0, 3 * SHARD)], x_s),
            (vb.at[:, 0], d_s),
            (hsend, h_s),
            (psend, p_s),
        ):
            remote(sent, sent, semaphore.at[0], rows_r.at[0], sibling).wait_send()

    def encode(source, lanes, target, top):
        step = jnp.ceil(FINE * jnp.log(jnp.maximum(top, 1e-36)))
        inverse = jnp.exp(step * (-1.0 / FINE))
        for r in range(0, 256, 64):
            value = source[pl.ds(r, 64), lanes]
            share = jnp.minimum(jnp.abs(value) * inverse, 1.0)
            root = share * lax.rsqrt(share + 1e-30) * FULL
            code = jnp.where(value < 0, -root, root)
            target[pl.ds(r, 64), :] = jnp.round(code).astype(jnp.int32).astype(jnp.int16)
        target[pl.ds(256, PAD), :] = jnp.broadcast_to(step, (PAD, UNIT)).astype(jnp.int32).astype(jnp.int16)

    def scale_of(message):
        step = message[pl.ds(256, PAD), :].astype(jnp.int32).astype(jnp.float32)
        return jnp.exp(step * (1.0 / FINE)) * (1.0 / (FULL * FULL))

    def decoded(message, r):
        code = message[pl.ds(r, 16), :].astype(jnp.int32).astype(jnp.float32)
        return code * jnp.abs(code)

    def fill_rows(source, dev):
        wide = source[...].astype(jnp.float32)
        for ch in range(2):
            part = wide[:, 8 * ch : 8 * ch + 8, :].reshape(64, 1024).astype(jnp.bfloat16)
            base = dev * 128
            a2[ch, base : base + 64, :] = part
            a2[ch, base + 64 : base + 128, :512] = part[:, 512:]
            a2[ch, base + 64 : base + 128, 512:] = -part[:, :512]

    def products(d):
        d_arrival(d).wait_recv()
        tops = []
        for ch in range(2):
            g = lax.dot_general(
                a2[ch], vb[d, ch], (((1,), (1,)), ((), ())), preferred_element_type=jnp.float32
            )
            gram[d, ch] = g
            tops.append(jnp.max(jnp.abs(g), axis=0, keepdims=True))
        for cr in range(2):
            lanes = slice(cr * UNIT, (cr + 1) * UNIT)
            for ch in range(2):
                top = jnp.max(tops[ch][:, lanes], keepdims=True)
                encode(gram.at[d, ch], pl.ds(cr * UNIT, UNIT), hsend.at[d, cr, ch], top)
            for ch in range(2):
                h_copy(d, ch, cr).start()

    def place(d, cr):
        there = (z - d + 8) % 8
        block = (there % 4) * 2 + (core if cr == 0 else 1 - core)
        return block, there // 4

    def smoothing(d):
        for cr in range(2):
            h_arrival(d, cr).wait_recv()
            top = jnp.zeros((16, 128), jnp.float32)
            lanes = pl.ds(cr * UNIT, UNIT)
            block, high = place(d, cr)
            first = pl.multiple_of(block * 512 + high * 256 + side * UNIT, UNIT)
            tile = block * 2 + high
            scale_next = scale_of(hrecv.at[d, cr, 0])
            scale_prev = scale_of(hrecv.at[d, cr, 1])
            for pair in range(4):
                taps = []
                for b in (2 * pair, 2 * pair + 1):
                    mine = 2 * b + row // 4
                    low = jnp.minimum(mine, tile)
                    spot = low * 16 - low * (low - 1) // 2 + jnp.abs(mine - tile)
                    owner = owner_ref[spot]
                    taps.append(
                        [[table_ref[k, owner, level_ref[ch]] * (1.0 / 512) for k in range(3)] for ch in range(2)]
                    )
                wide = [
                    [
                        jnp.concatenate(
                            [jnp.full((8, 128), taps[0][ch][k]), jnp.full((8, 128), taps[1][ch][k])], axis=0
                        )
                        for k in range(3)
                    ]
                    for ch in range(2)
                ]
                wide_prev = jnp.where(freq > 0, wide[0][0] * scale_prev, 0.0)
                wide_next = jnp.where(freq < freq_count - 1, wide[1][2] * scale_next, 0.0)
                for dev in range(2):
                    for part in range(2):
                        r = (dev * 2 + part) * 64 + pair * 16
                        g0 = gram[d, 0, pl.ds(r, 16), lanes]
                        g1 = gram[d, 1, pl.ds(r, 16), lanes]
                        before = decoded(hrecv.at[d, cr, 1], r)
                        after = decoded(hrecv.at[d, cr, 0], r)
                        f0 = wide_prev * before + wide[0][1] * g0 + wide[0][2] * g1
                        f1 = wide[1][0] * g0 + wide[1][1] * g1 + wide_next * after
                        if dev == 0:
                            for ch, value in ((0, f0), (1, f1)):
                                out_ref[ch, part, 2 * pair : 2 * pair + 2, 0, :, pl.ds(first, UNIT)] = (
                                    value.reshape(2, 8, 128)
                                )
                        else:
                            for ch, value in ((0, f0), (1, f1)):
                                smooth[pl.ds((ch * 2 + part) * 64 + pair * 16, 16), :] = value
                            top = jnp.maximum(top, jnp.maximum(jnp.abs(f0), jnp.abs(f1)))
            encode(smooth, slice(None), psend.at[d, cr], jnp.max(top, keepdims=True))
            p_copy(d, cr).start()

    def delivery(d):
        p_arrival(d).wait_recv()
        for cr in range(2):
            block, high = place(d, cr)
            first = pl.multiple_of(block * 512 + high * 256 + (1 - side) * UNIT, UNIT)
            scale = scale_of(precv.at[d, cr])
            for ch in range(2):
                for part in range(2):
                    for pair in range(4):
                        value = decoded(precv.at[d, cr], (ch * 2 + part) * 64 + pair * 16) * scale
                        out_ref[ch, part, 2 * pair : 2 * pair + 2, 0, :, pl.ds(first, UNIT)] = (
                            value.reshape(2, 8, 128)
                        )

    fetches = [
        pltpu.make_async_copy(v_hbm.at[ch], vb.at[0, ch, pl.ds(own_half, SHARD)], in_s.at[ch]) for ch in range(2)
    ]
    fetches.append(pltpu.make_async_copy(owner_hbm, owner_ref, in_s.at[2]))
    fetches.append(pltpu.make_async_copy(level_hbm, level_ref, in_s.at[3]))
    fetches.append(pltpu.make_async_copy(table_hbm, table_ref, in_s.at[4]))
    for fetch in fetches:
        fetch.start()

    barrier = pltpu.get_barrier_semaphore()
    for device in (z_next, z_prev, x_mate, p_mate, sibling, f_next, f_prev):
        pl.semaphore_signal(barrier, inc=1, device_id=device, device_id_type=MESH)
    for turn in range(8):
        b = (col + 8 - turn) % 8

        @pl.when(jnp.logical_not(jnp.logical_and(diagonal, turn == 0)))
        def _():
            pl.semaphore_signal(barrier, inc=1, device_id=(b, row, freq), device_id_type=MESH)

    for fetch in fetches:
        fetch.wait()

    own = [vb[0, ch, pl.ds(own_half, SHARD), :].astype(jnp.float32) for ch in range(2)]
    for c in range(8):
        pieces = [own[ch][8 * c : 8 * c + 8, :] for ch in range(2)]
        stripes[c] = jnp.concatenate(pieces, axis=0).astype(jnp.bfloat16)

    pl.semaphore_wait(barrier, 15 - jnp.where(diagonal, 1, 0))

    @pl.when(diagonal)
    def _():
        rows_own[row] = stripes[col]

    for name in FIRST:
        if name == "r":
            for turn in range(8):
                c = (row + turn) % 8

                @pl.when(jnp.logical_not(jnp.logical_and(diagonal, turn == 0)))
                def _():
                    row_copy(c).start()
        elif name in "xv":
            x_copy(0, "xv".index(name)).start()
            d_copy(0, "xv".index(name), own_half).start()
        else:
            for way in range(2):
                z_copy(way, 0 if name == "a" else 2, 1).start()

    def units(t):
        return [t, 8 - t] if t < 4 else [4]

    def ring(stream, t):
        for way in range(2):
            if t < 4 or stream == 2 or way == stream:
                z_copy(way, stream, t).wait_recv()
                if t < 3 or (t == 3 and (stream == 2 or way == stream)):
                    z_copy(way, stream, t + 1).start()
                if t < 4 or stream < 2 or way == 1:
                    d = units(t)[way if t < 4 else 0]
                    if stream == 2:
                        x_copy(d, 1).start()
                    d_copy(d, stream // 2, mate_half if stream == 1 else own_half).start()

    def step(kind, t):
        if kind == "C":
            ring(2, t)
        elif kind == "A":
            ring(0, t)
        elif kind == "B":
            ring(1, t)
        elif kind in "XY":
            d = t if kind == "X" else 8 - t
            x_arrival(d, 1).wait_recv()
            d_copy(d, 1, mate_half).start()
        elif kind == "R":
            for turn in range(8):
                b = (col + 8 - turn) % 8

                @pl.when(jnp.logical_not(jnp.logical_and(diagonal, turn == 0)))
                def _():
                    row_arrival(b).wait_recv()
                mate_copy(b).start()
            fill_rows(rows_own, 0)
        elif kind == "M":
            remote(rows_own, rows_mate, mate_s.at[0], mate_r.at[0], p_mate).wait_recv()
            fill_rows(rows_mate, 1)
        elif kind == "I":
            x_arrival(0, t).wait_recv()
            if t == 0:
                for way in range(2):
                    z_copy(way, 1, 1).start()
            d_copy(0, t, mate_half).start()
        elif kind == "g":
            products(t)
        elif kind == "f":
            smoothing(t)
        elif kind == "o":
            delivery(t)

    for group in ORDER:
        for name in group.split():
            step(name[0], int(name[1]))
    all_left()


def on_device(voltages, pair_owner, chan_level, stencil_table):
    operands = (voltages, pair_owner, chan_level, jnp.transpose(stencil_table, (2, 0, 1)))
    anywhere = pl.BlockSpec(memory_space=pltpu.HBM)
    dma = pltpu.SemaphoreType.DMA
    return pl.pallas_call(
        correlator_kernel,
        out_shape=pltpu.VMEM((2, 2, 8, 1, 8, 4096), jnp.float32),
        in_specs=[anywhere] * 4,
        out_specs=pl.BlockSpec(memory_space=pltpu.VMEM),
        scratch_shapes=[
            pltpu.SMEM((136,), jnp.int32),
            pltpu.SMEM((2,), jnp.int32),
            pltpu.SMEM((3, 4, 8), jnp.float32),
            pltpu.VMEM((8, 2, 256, 1024), jnp.bfloat16),
            pltpu.VMEM((8, 16, 1024), jnp.bfloat16),
            pltpu.VMEM((8, 16, 1024), jnp.bfloat16),
            pltpu.VMEM((8, 16, 1024), jnp.bfloat16),
            pltpu.VMEM((2, 256, 1024), jnp.bfloat16),
            pltpu.VMEM((8, 2, 256, 256), jnp.float32),
            pltpu.VMEM((256, UNIT), jnp.float32),
            pltpu.VMEM((8, 2, 2, 256 + PAD, UNIT), jnp.int16),
            pltpu.VMEM((8, 2, 2, 256 + PAD, UNIT), jnp.int16),
            pltpu.VMEM((8, 2, 256 + PAD, UNIT), jnp.int16),
            pltpu.VMEM((8, 2, 256 + PAD, UNIT), jnp.int16),
            dma((5,)), dma((1,)), dma((8,)), dma((1,)), dma((1,)),
            dma((1,)), dma((2, 3, 4)),
            dma((1,)), dma((9,)),
            dma((1,)), dma((8,)),
            dma((1,)), dma((8, 2)),
            dma((1,)), dma((8,)),
        ],
        compiler_params=pltpu.CompilerParams(
            collective_id=0, has_side_effects=True, vmem_limit_bytes=44 * 1024 * 1024
        ),
    )(*(pltpu.with_memory_space_constraint(each, pltpu.HBM) for each in operands))


def solution(mesh):
    in_specs = (P("freq", ("row", "col"), None), P(), P("freq"), P())
    out_specs = P("freq", None, None, ("row", "col"), None, None)
    return jax.shard_map(
        on_device, mesh=mesh, in_specs=in_specs, out_specs=out_specs, check_vma=False
    )
```
